512 devices in a mesh: lon: 32 (over z_lo, y, core), lat: 16 (over z_hi, x).
Axes of the slice: x: 4, y: 8, z: 8 (z_hi: 4, z_lo: 2; z = z_hi * 2 + z_lo), core: 2. Of those that a mesh axis runs over, the one named last changes fastest.
Arguments:
- latent: bfloat16 [2, 192, 1536, 512], P(None, 'lat', 'lon'), may hold values from -6 to 6
- w_qkv: bfloat16 [512, 1536], replicated, may hold values from -0.25 to 0.25
- w_out: bfloat16 [512, 512], replicated, may hold values from -0.25 to 0.25
- b_out: float32 [512], replicated, may hold values from -3 to 3
- norm_gain: float32 [512], replicated, may hold values from 0.25 to 1.75
- norm_shift: float32 [512], replicated, may hold values from -2 to 2
- earth_bias: bfloat16 [32, 8, 144, 144], P('lat'), may hold values from -4 to 324
Outputs:
- updated: bfloat16 [2, 192, 1536, 512], P(None, 'lat', 'lon')
The draws below stay inside these ranges and needn't reach their ends.
All inputs are finite; a program needn't handle non-finite values.
Results may differ from the reference program's by a relative error of at most 0.011.
Values may be sent and summed in bfloat16 or wider, within the bound.
A program may use at most 128 MiB of HBM per device.

```python
import jax
import jax.numpy as jnp
from jax import lax

D = 512
HEADS = 8
HEAD_DIM = 64
LEV = 2
WLAT = 6
WLON = 12
SLAT = 3
SLON = 6
WT = 144
NLAT = 192
NLON = 1536
NWLAT = 32


def draw_earth_bias(key, part):
    key = jax.random.fold_in(key, 7)
    keys = jax.random.split(key, 1)
    shape = (NWLAT, HEADS, WT, WT)
    values = jnp.clip(jax.random.normal(keys[0], shape, jnp.float32), -4.0, 4.0)
    return values.astype(jnp.bfloat16)


def level_of(own_key, extent, shards, smallest, largest):
    level = 1.0
    for position, shards_of in shards:
        draws = jax.random.uniform(jax.random.fold_in(jax.random.fold_in(own_key, 6), position), (shards_of,), jnp.float32, smallest / len(shards), largest / len(shards))
        level = level * jnp.repeat(jnp.exp(draws), extent[position] // shards_of).reshape((-1,) + (1,) * (len(extent) - 1 - position))
    return level


def scatter_about(own_key, extent, scale, reach, shards=(), kind=jnp.bfloat16):
    loudness = level_of(own_key, extent, shards, -0.22, 0.18) if shards else 1.0
    values = jax.random.normal(own_key, extent, jnp.float32) * scale * loudness
    return jnp.minimum(jnp.maximum(values, -reach), reach).astype(kind)


def setup_inputs(seed: int = 0) -> dict:
    arg_keys = jax.random.split(jax.random.key(seed), 8)
    return {
        "latent": scatter_about(arg_keys[0], (LEV, NLAT, NLON, D), 1.0, 6.0, ((1, 16), (2, 32))),
        "w_qkv": scatter_about(arg_keys[1], (D, 3 * D), D ** -0.5, 0.25),
        "w_out": scatter_about(arg_keys[2], (D, D), D ** -0.5, 0.25),
        "b_out": scatter_about(arg_keys[3], (D,), 0.5, 3.0, (), jnp.float32),
        "norm_gain": jnp.clip(1.0 + 0.15 * jax.random.normal(arg_keys[4], (D,), jnp.float32), 0.25, 1.75),
        "norm_shift": scatter_about(arg_keys[5], (D,), 0.3, 2.0, (), jnp.float32),
        "earth_bias": draw_earth_bias(jax.random.fold_in(arg_keys[7], 71), 0),
    }


def attend_band(band, bias_rows, is_last, w_qkv, w_out, b_out):
    nwo = NLON // WLON
    qkv = jnp.dot(band.reshape(-1, D), w_qkv, preferred_element_type=jnp.float32).astype(jnp.bfloat16)
    qkv = qkv.reshape(LEV, WLAT, nwo, WLON, 3, HEADS, HEAD_DIM)
    wins = qkv.transpose(2, 0, 1, 3, 4, 5, 6).reshape(nwo, WT, 3, HEADS, HEAD_DIM).astype(jnp.float32)
    query, keys, values = (wins[:, :, 0], wins[:, :, 1], wins[:, :, 2])
    scores = jnp.einsum('wqhe,wkhe->whqk', query, keys) / jnp.sqrt(jnp.float32(HEAD_DIM))
    scores = scores + bias_rows.astype(jnp.float32)[None]
    latrow = jnp.arange(WT) // WLON % WLAT
    group = jnp.logical_and(is_last, latrow >= WLAT - SLAT)
    allowed = group[:, None] == group[None, :]
    scores = jnp.where(allowed[None, None], scores, jnp.float32(-1e+30))
    probs = jax.nn.softmax(scores, axis=-1).astype(jnp.bfloat16)
    attended = jnp.einsum('whqk,wkhe->wqhe', probs.astype(jnp.float32), values).astype(jnp.bfloat16)
    attended = attended.reshape(nwo * WT, D)
    projected = (jnp.dot(attended, w_out, preferred_element_type=jnp.float32) + b_out).astype(jnp.bfloat16)
    projected = projected.reshape(nwo, LEV, WLAT, WLON, D).transpose(1, 2, 0, 3, 4)
    return projected.reshape(LEV, WLAT, NLON, D)

def reference(latent, w_qkv, w_out, b_out, norm_gain, norm_shift, earth_bias):
    shifted = jnp.roll(latent, (-SLAT, -SLON), axis=(1, 2))
    bands = shifted.reshape(LEV, NWLAT, WLAT, NLON, D).transpose(1, 0, 2, 3, 4)
    index = jnp.arange(NWLAT, dtype=jnp.int32)

    def one_band(packed):
        band, bias_rows, row_index = packed
        return attend_band(band, bias_rows, row_index == NWLAT - 1, w_qkv, w_out, b_out)
    projected = lax.map(one_band, (bands, earth_bias, index))
    projected = projected.transpose(1, 0, 2, 3, 4).reshape(LEV, NLAT, NLON, D)
    returned = jnp.roll(projected, (SLAT, SLON), axis=(1, 2)).astype(jnp.float32)
    mean = lax.optimization_barrier(jnp.mean(returned, axis=-1, keepdims=True))
    var = lax.optimization_barrier(jnp.mean((returned - mean) ** 2, axis=-1, keepdims=True))
    normed = (returned - mean) / jnp.sqrt(var + 1e-05) * norm_gain + norm_shift
    return (latent.astype(jnp.float32) + normed).astype(jnp.bfloat16)
```

```python
import functools

import jax
import jax.numpy as jnp
from jax import lax
from jax.experimental import pallas as pl
from jax.experimental.pallas import tpu as pltpu
from jax.sharding import PartitionSpec as P

LEV = 2
WLAT = 6
WLON = 12
SLAT = 3
SLON = 6
WT = 144
HEADS = 8
D = 512
LT = 4
F32 = jnp.float32
BF16 = jnp.bfloat16
MESH = pl.DeviceIdType.MESH

(C_LAT_M, C_LAT_S, C_LAT_N, C_WQKV, C_WOUT, C_BIAS, C_OUT_M, C_OUT_S, C_OUT_N) = range(9)
(R_EM, R_ES, R_S0, R_S1, R_S2, R_COR, R_RM, R_RS, R_R0, R_R1, R_R2, R_RC, R_RD) = range(13)


def split_tiles(value):
    return [value[..., 128 * t : 128 * (t + 1)] for t in range(LT)]


def kernel(
    nlat, nlon,
    lat_h, wqkv_h, wout_h, b_out, gain, shift, bias_h, out_h,
    lat_v, wqkv, wout, bias_v, biasf, fx, pf, win_in, win_out, cmp_f,
    ehalo, shalo, chalo, s80, s48, r80, r48, out_v,
    lsem, ssem, rsem,
):
    ilat, ilon = lax.axis_index("lat"), lax.axis_index("lon")
    north = lax.rem(ilat + nlat - 1, nlat)
    south = lax.rem(ilat + 1, nlat)
    west = lax.rem(ilon + nlon - 1, nlon)
    east = lax.rem(ilon + 1, nlon)
    to_n = {"lat": north, "lon": ilon}
    to_s = {"lat": south, "lon": ilon}
    to_w = {"lat": ilat, "lon": west}
    to_e = {"lat": ilat, "lon": east}
    to_nw = {"lat": north, "lon": west}
    to_se = {"lat": south, "lon": east}

    barrier = pltpu.get_barrier_semaphore()
    for who in (to_n, to_s, to_w, to_e, to_nw, to_se):
        pl.semaphore_signal(barrier, inc=1, device_id=who, device_id_type=MESH)

    def local(src, dst, which):
        return pltpu.make_async_copy(src, dst, lsem.at[which])

    def remote(src, dst, which, who):
        return pltpu.make_async_remote_copy(
            src_ref=src, dst_ref=dst, send_sem=ssem.at[which], recv_sem=rsem.at[which],
            device_id=who, device_id_type=MESH,
        )

    loads = {
        C_LAT_M: local(lat_h.at[:, 3:9], lat_v.at[:, 3:9], C_LAT_M),
        C_WQKV: local(wqkv_h, wqkv, C_WQKV),
        C_BIAS: local(bias_h, bias_v, C_BIAS),
        C_WOUT: local(wout_h, wout, C_WOUT),
        C_LAT_S: local(lat_h.at[:, 9:12], lat_v.at[:, 9:12], C_LAT_S),
        C_LAT_N: local(lat_h.at[:, 0:3], lat_v.at[:, 0:3], C_LAT_N),
    }
    for copy in loads.values():
        copy.start()

    sends = {
        R_S0: remote(lat_h.at[:, 0:3, 0:16], shalo.at[0], R_S0, to_n),
        R_EM: remote(lat_h.at[:, 3:9, 0:16], ehalo.at[:, 0:6], R_EM, to_w),
        R_S1: remote(lat_h.at[:, 0:3, 16:32], shalo.at[1], R_S1, to_n),
        R_S2: remote(lat_h.at[:, 0:3, 32:48], shalo.at[2], R_S2, to_n),
        R_ES: remote(lat_h.at[:, 9:12, 0:16], ehalo.at[:, 6:9], R_ES, to_w),
        R_COR: remote(shalo.at[0], chalo, R_COR, to_w),
        R_RM: remote(s80.at[3], r80.at[3], R_RM, to_e),
        R_RS: remote(s48.at[0], r48.at[0], R_RS, to_e),
        R_R0: remote(s80.at[0], r80.at[0], R_R0, to_s),
        R_R1: remote(s80.at[1], r80.at[1], R_R1, to_s),
        R_R2: remote(s80.at[2], r80.at[2], R_R2, to_s),
        R_RC: remote(s48.at[1], r48.at[1], R_RC, to_s),
        R_RD: remote(s48.at[2], r48.at[2], R_RD, to_se),
    }
    pl.semaphore_wait(barrier, 6)
    for which in (R_S0, R_EM, R_S1, R_S2, R_ES):
        sends[which].start()

    loads[C_BIAS].wait()
    is_last = ilat == nlat - 1

    def south_half(axis):
        at = lax.broadcasted_iota(jnp.int32, (WT, WT), axis)
        return jnp.logical_or(jnp.logical_and(at >= 36, at < 72), at >= 108)

    apart = jnp.logical_and(south_half(0) != south_half(1), is_last)
    penalty = jnp.where(apart, F32(-1e30), F32(0.0))
    for r in range(2):
        for h in range(HEADS):
            value = bias_v[r, h].astype(F32)
            biasf[r, h // 2, WT * (h % 2) : WT * (h % 2 + 1), :] = value + penalty if r else value

    lane = lax.broadcasted_iota(jnp.int32, (1, 128), 1)
    first = lane < 64
    scale0 = jnp.where(first, F32(0.125), F32(0.0))
    scale1 = jnp.where(first, F32(0.0), F32(0.125))

    def spread(value, dst):
        for t, tile in enumerate(split_tiles(value)):
            dst[t][...] = tile.astype(F32)

    def attend(r, x):
        qkv = jnp.dot(x, wqkv[...], preferred_element_type=F32)
        parts = []
        for p in range(HEADS // 2):
            qf = qkv[:, 128 * p : 128 * (p + 1)]
            kp = qkv[:, D + 128 * p : D + 128 * (p + 1)].astype(BF16)
            vp = qkv[:, 2 * D + 128 * p : 2 * D + 128 * (p + 1)].astype(BF16)
            q2 = jnp.concatenate([(qf * scale0).astype(BF16), (qf * scale1).astype(BF16)], 0)
            s = lax.dot_general(q2, kp, (((1,), (1,)), ((), ())), preferred_element_type=F32)
            s = s + biasf[r, p]
            e = jnp.exp(s - jnp.max(s, axis=-1, keepdims=True)).astype(BF16)
            vx = jnp.concatenate([vp, jnp.ones((WT, 128), BF16)], 1)
            o = jnp.dot(e, vx, preferred_element_type=F32)
            num = jnp.where(first, o[:WT, :128], o[WT:, :128])
            den = jnp.where(first, o[:WT, 128:], o[WT:, 128:])
            parts.append((num / den).astype(BF16))
        att = jnp.concatenate(parts, 1)
        proj = jnp.dot(att, wout[...], preferred_element_type=F32) + b_out[...]
        return proj.astype(BF16).astype(F32)

    def compact(rows_of, dst, width, at):
        slot = cmp_f.at[at]
        for n, row in enumerate(rows_of):
            slot[:, width * n : width * (n + 1), :] = win_out[at, :, row : row + width, :]
        size = dst.shape[0]
        for t in range(LT):
            dst[:, 128 * t : 128 * (t + 1)] = slot[t, 0:size, :].astype(BF16)

    def window(r, b):
        at = b % 2
        for l in range(LEV):
            for i in range(WLAT):
                j = WLON * (WLAT * l + i)
                win_in[at, :, j : j + WLON, :] = fx[
                    :, l, WLAT * r + i, SLON + WLON * b : SLON + WLON * (b + 1), :
                ]
        x = jnp.concatenate([win_in[at, t].astype(BF16) for t in range(LT)], 1)
        proj = attend(r, x)
        for t, tile in enumerate(split_tiles(proj)):
            win_out[at, t] = tile
        own = WLON if b < 3 else SLON
        for l in range(LEV):
            for i in range(WLAT if r == 0 else SLAT):
                j = WLON * (WLAT * l + i)
                pf[:, l, 3 + WLAT * r + i, SLON + WLON * b : SLON + WLON * b + own, :] = win_out[
                    at, :, j : j + own, :
                ]
        at_row = lambda l, i: WLON * (WLAT * l + i)
        if r == 0 and b == 3:
            compact([at_row(l, i) + SLON for l in range(LEV) for i in range(WLAT)], s80.at[3], SLON, at)
            sends[R_RM].start()
        if r == 1 and b < 3:
            compact([at_row(l, i) for l in range(LEV) for i in range(SLAT, WLAT)], s80.at[b], WLON, at)
            sends[R_R0 + b].start()
        if r == 1 and b == 3:
            low = [(l, i) for l in range(LEV) for i in range(SLAT, WLAT)]
            compact([at_row(l, i) + SLON for l, i in low], s48.at[2], SLON, at)
            sends[R_RD].start()
            compact([at_row(l, i) for l, i in low], s48.at[1], SLON, at)
            sends[R_RC].start()
            high = [(l, i) for l in range(LEV) for i in range(SLAT)]
            compact([at_row(l, i) + SLON for l, i in high], s48.at[0], SLON, at)
            sends[R_RS].start()

    def unpack(src, width, at, places):
        slot = cmp_f.at[at]
        size = src.shape[0]
        for t in range(LT):
            slot[t, 0:size, :] = src[:, 128 * t : 128 * (t + 1)].astype(F32)
        for n, (l, row, col) in enumerate(places):
            pf[:, l, row, col : col + width, :] = slot[:, width * n : width * (n + 1), :]

    def finish(row0, row1):
        for l in range(LEV):
            for row in range(row0, row1):
                v = jnp.concatenate([pf[t, l, row] for t in range(LT)], 1)
                mean = jnp.mean(v, axis=-1, keepdims=True)
                d = v - mean
                var = jnp.mean(d * d, axis=-1, keepdims=True)
                normed = d * lax.rsqrt(var + F32(1e-5)) * gain[...] + shift[...]
                out_v[l, row] = (lat_v[l, row].astype(F32) + normed).astype(BF16)

    loads[C_LAT_M].wait()
    for l in range(LEV):
        for i in range(6):
            spread(lat_v[l, 3 + i], [fx.at[t, l, i, 0:48] for t in range(LT)])
    loads[C_WQKV].wait()
    loads[C_WOUT].wait()
    for b in range(3):
        window(0, b)
    sends[R_EM].wait_recv()
    for l in range(LEV):
        for i in range(6):
            spread(ehalo[l, i], [fx.at[t, l, i, 48:64] for t in range(LT)])
    window(0, 3)

    loads[C_LAT_S].wait()
    for l in range(LEV):
        for i in range(3):
            spread(lat_v[l, 9 + i], [fx.at[t, l, 6 + i, 0:48] for t in range(LT)])

    def take_south(p):
        for l in range(LEV):
            for i in range(3):
                spread(shalo[p, l, i], [fx.at[t, l, 9 + i, 16 * p : 16 * (p + 1)] for t in range(LT)])

    sends[R_S0].wait_recv()
    sends[R_COR].start()
    take_south(0)
    sends[R_S1].wait_recv()
    take_south(1)
    window(1, 0)
    window(1, 1)
    sends[R_S2].wait_recv()
    take_south(2)
    window(1, 2)
    sends[R_ES].wait_recv()
    sends[R_COR].wait_recv()
    for l in range(LEV):
        for i in range(3):
            spread(ehalo[l, 6 + i], [fx.at[t, l, 6 + i, 48:64] for t in range(LT)])
            spread(chalo[l, i], [fx.at[t, l, 9 + i, 48:64] for t in range(LT)])
    window(1, 3)

    sends[R_RM].wait_recv()
    unpack(r80.at[3], SLON, 0, [(l, 3 + i, 0) for l in range(LEV) for i in range(WLAT)])
    finish(3, 9)
    out_m = local(out_v.at[:, 3:9], out_h.at[:, 3:9], C_OUT_M)
    out_m.start()
    loads[C_LAT_N].wait()
    sends[R_RS].wait_recv()
    unpack(r48.at[0], SLON, 1, [(l, 9 + i, 0) for l in range(LEV) for i in range(SLAT)])
    finish(9, 12)
    out_s = local(out_v.at[:, 9:12], out_h.at[:, 9:12], C_OUT_S)
    out_s.start()
    for b in range(3):
        sends[R_R0 + b].wait_recv()
        unpack(
            r80.at[b], WLON, b % 2,
            [(l, i, SLON + WLON * b) for l in range(LEV) for i in range(SLAT)],
        )
    sends[R_RC].wait_recv()
    unpack(r48.at[1], SLON, 1, [(l, i, 42) for l in range(LEV) for i in range(SLAT)])
    sends[R_RD].wait_recv()
    unpack(r48.at[2], SLON, 0, [(l, i, 0) for l in range(LEV) for i in range(SLAT)])
    finish(0, 3)
    out_n = local(out_v.at[:, 0:3], out_h.at[:, 0:3], C_OUT_N)
    out_n.start()
    for copy in sends.values():
        copy.wait_send()
    out_m.wait()
    out_s.wait()
    out_n.wait()


def local_step(nlat, nlon, latent, w_qkv, w_out, b_out, norm_gain, norm_shift, earth_bias):
    hbm = pl.BlockSpec(memory_space=pl.ANY)
    vmem = pl.BlockSpec(memory_space=pltpu.VMEM)
    tile = latent.shape
    return pl.pallas_call(
        functools.partial(kernel, nlat, nlon),
        out_shape=jax.ShapeDtypeStruct(tile, BF16),
        in_specs=[hbm, hbm, hbm, vmem, vmem, vmem, hbm],
        out_specs=hbm,
        scratch_shapes=[
            pltpu.VMEM(tile, BF16),
            pltpu.VMEM((D, 3 * D), BF16),
            pltpu.VMEM((D, D), BF16),
            pltpu.VMEM((2, HEADS, WT, WT), BF16),
            pltpu.VMEM((2, HEADS // 2, 2 * WT, WT), F32),
            pltpu.VMEM((LT, LEV, 12, 64, 128), F32),
            pltpu.VMEM((LT, LEV, 12, 48, 128), F32),
            pltpu.VMEM((2, LT, WT, 128), F32),
            pltpu.VMEM((2, LT, WT, 128), F32),
            pltpu.VMEM((2, LT, 80, 128), F32),
            pltpu.VMEM((LEV, 9, 16, D), BF16),
            pltpu.VMEM((3, LEV, 3, 16, D), BF16),
            pltpu.VMEM((LEV, 3, 16, D), BF16),
            pltpu.VMEM((4, 80, D), BF16),
            pltpu.VMEM((3, 48, D), BF16),
            pltpu.VMEM((4, 80, D), BF16),
            pltpu.VMEM((3, 48, D), BF16),
            pltpu.VMEM(tile, BF16),
            pltpu.SemaphoreType.DMA((9,)),
            pltpu.SemaphoreType.DMA((13,)),
            pltpu.SemaphoreType.DMA((13,)),
        ],
        compiler_params=pltpu.CompilerParams(
            collective_id=0, has_side_effects=True, vmem_limit_bytes=48 * 1024 * 1024
        ),
        name="swin_window_attention",
    )(
        latent, w_qkv, w_out, b_out.reshape(1, D), norm_gain.reshape(1, D),
        norm_shift.reshape(1, D), earth_bias,
    )


def solution(mesh):
    placed = (P(None, "lat", "lon", None), P(), P(), P(), P(), P(), P("lat", None, None, None))
    step = functools.partial(local_step, mesh.shape["lat"], mesh.shape["lon"])
    return jax.shard_map(
        step, mesh=mesh, in_specs=placed, out_specs=P(None, "lat", "lon", None), check_vma=False
    )
```

```python
import functools

import jax
import jax.numpy as jnp
from jax import lax
from jax.experimental import pallas as pl
from jax.experimental.pallas import tpu as pltpu
from jax.sharding import PartitionSpec as P

LEV = 2
WLAT = 6
WLON = 12
SLAT = 3
SLON = 6
WT = 144
HEADS = 8
D = 512
LT = 4
GROUP = 4
F32 = jnp.float32
BF16 = jnp.bfloat16
MESH = pl.DeviceIdType.MESH

(C_N, C_M, C_S, C_WQKV, C_WOUT, C_BIAS, C_B, C_G, C_H) = range(9)
XA, XB, XR, XF, RA, RB, RR, RF = range(0, 32, 4)
EM, ES, COR, WM, WS, DIAG = range(32, 38)
COPIES = 38

X_CUTS = ((0, 48, 80), (80, 128, 160), (160, 192, 224), (224, 256, 288))
X_CORNER_E = 36
X_WINDOW = 72
R_CUTS = ((0, 16, 32), (32, 64, 96), (96, 144, 176), (176, 224, 256))
R_WINDOW = 36


def kernel(
    nlat, nlon,
    lat_h, wqkv_h, wout_h, b_h, gain_h, shift_h, bias_h, out_v,
    lat_v, wqkv, wout, b_out, gain, shift, bias_v, biasf, fx, pf, win_in, win_out,
    stage, stage_r, xs, xr, xrelay, rs, rr, rrelay, cmp_f, s80, s48, r80, r48, cor,
    lsem, ssem, rsem,
):
    ilat, ilon = lax.axis_index("lat"), lax.axis_index("lon")

    def at(dlat, dlon):
        return {
            "lat": lax.rem(ilat + dlat + nlat, nlat),
            "lon": lax.rem(ilon + dlon + nlon, nlon),
        }

    place = lax.rem(ilat, GROUP)
    head, tail = place == 0, place == GROUP - 1
    inner = jnp.logical_and(place != 0, place != GROUP - 1)

    barrier = pltpu.get_barrier_semaphore()

    def greet(who):
        pl.semaphore_signal(barrier, inc=1, device_id=who, device_id_type=MESH)

    for who in (at(-1, 0), at(1, 0), at(0, -1), at(0, 1), at(-1, -1), at(1, 1)):
        greet(who)

    @pl.when(head)
    def _():
        for who in (at(GROUP - 1, 0), at(GROUP, 0), at(-GROUP, 0)):
            greet(who)

    @pl.when(tail)
    def _():
        for who in (at(1 - GROUP, 0), at(GROUP, 0), at(-GROUP, 0)):
            greet(who)

    def local(src, dst, which):
        return pltpu.make_async_copy(src, dst, lsem.at[which])

    def remote(src, dst, which, who, send=None):
        return pltpu.make_async_remote_copy(
            src_ref=src, dst_ref=dst, send_sem=ssem.at[which if send is None else send],
            recv_sem=rsem.at[which], device_id=who, device_id_type=MESH,
        )

    loads = {
        C_N: local(lat_h.at[:, 0:3], lat_v.at[:, 0:3], C_N),
        C_M: local(lat_h.at[:, 3:9], lat_v.at[:, 3:9], C_M),
        C_S: local(lat_h.at[:, 9:12], lat_v.at[:, 9:12], C_S),
        C_BIAS: local(bias_h, bias_v, C_BIAS),
        C_WQKV: local(wqkv_h, wqkv, C_WQKV),
        C_WOUT: local(wout_h, wout, C_WOUT),
        C_B: local(b_h, b_out, C_B),
        C_G: local(gain_h, gain, C_G),
        C_H: local(shift_h, shift, C_H),
    }
    for copy in loads.values():
        copy.start()

    def rows(ref, a, b):
        return ref.at[a:b]

    def x_direct(k):
        a, m, _ = X_CUTS[k]
        return remote(rows(xs, a, m), rows(xr, a, m), XA + k, at(-1, 0))

    def x_other(k):
        _, m, b = X_CUTS[k]
        return remote(rows(xs, m, b), rows(xr, m, b), XB + k, at(-1, 0))

    def x_around(k):
        _, m, b = X_CUTS[k]
        return remote(rows(xs, m, b), rows(xrelay, m, b), XR + k, at(GROUP - 1, 0), XB + k)

    def x_forward(k):
        _, m, b = X_CUTS[k]
        return remote(rows(xrelay, m, b), rows(xr, m, b), XB + k, at(-GROUP, 0), XF + k)

    def r_direct(k):
        a, m, _ = R_CUTS[k]
        return remote(rows(rs, a, m), rows(rr, a, m), RA + k, at(1, 0))

    def r_other(k):
        _, m, b = R_CUTS[k]
        return remote(rows(rs, m, b), rows(rr, m, b), RB + k, at(1, 0))

    def r_around(k):
        _, m, b = R_CUTS[k]
        return remote(rows(rs, m, b), rows(rrelay, m, b), RR + k, at(1 - GROUP, 0), RB + k)

    def r_forward(k):
        _, m, b = R_CUTS[k]
        return remote(rows(rrelay, m, b), rows(rr, m, b), RB + k, at(GROUP, 0), RF + k)

    def x_send(k):
        pl.when(head)(x_around(k).start)
        pl.when(jnp.logical_not(head))(x_other(k).start)
        x_direct(k).start()

    def r_send(k):
        pl.when(tail)(r_around(k).start)
        pl.when(jnp.logical_not(tail))(r_other(k).start)
        r_direct(k).start()

    def x_relay(k):
        @pl.when(tail)
        def _():
            x_around(k).wait_recv()
            x_forward(k).start()

    def r_relay(k):
        @pl.when(head)
        def _():
            r_around(k).wait_recv()
            r_forward(k).start()

    em = remote(s80.at[0], r80.at[0], EM, at(0, -1))
    es = remote(s48.at[0], r48.at[0], ES, at(0, -1))
    corner = remote(rows(xr, 0, 48), cor, COR, at(0, -1))
    wm = remote(s80.at[1], r80.at[1], WM, at(0, 1))
    ws = remote(s48.at[1], r48.at[1], WS, at(0, 1))
    diag = remote(s48.at[2], r48.at[2], DIAG, at(1, 1))

    def widen(src, dst, a, b):
        for t in range(LT):
            dst[t, a:b, :] = src[a:b, 128 * t : 128 * (t + 1)].astype(F32)

    def narrow(src, dst, a, b):
        for t in range(LT):
            dst[a:b, 128 * t : 128 * (t + 1)] = src[t, a:b, :].astype(BF16)

    def spread(row0, row1):
        for l in range(LEV):
            for row in range(row0, row1):
                for t in range(LT):
                    fx[t, l, row, 0:48] = lat_v[l, row, :, 128 * t : 128 * (t + 1)].astype(F32)

    loads[C_N].wait()
    spread(0, 3)
    n = 0
    for col, width in ((0, 6), (42, 6), (6, 12), (18, 12), (30, 12)):
        for l in range(LEV):
            for i in range(SLAT):
                stage[:, n : n + width, :] = fx[:, l, i, col : col + width, :]
                n += width
    narrow(stage, xs, 0, 288)

    loads[C_M].wait()
    spread(3, 9)
    n = 0
    for l in range(LEV):
        for row in range(3, 9):
            cmp_f[0, :, n : n + SLON, :] = fx[:, l, row, 0:SLON, :]
            n += SLON
    narrow(cmp_f.at[0], s80.at[0], 0, 80)
    loads[C_S].wait()
    spread(9, 12)
    n = 0
    for l in range(LEV):
        for row in range(9, 12):
            cmp_f[1, :, n : n + SLON, :] = fx[:, l, row, 0:SLON, :]
            n += SLON
    narrow(cmp_f.at[1], s48.at[0], 0, 48)

    loads[C_BIAS].wait()
    is_last = ilat == nlat - 1

    def south_half(axis):
        n = lax.broadcasted_iota(jnp.int32, (WT, WT), axis)
        return jnp.logical_or(jnp.logical_and(n >= 36, n < 72), n >= 108)

    apart = jnp.logical_and(south_half(0) != south_half(1), is_last)
    penalty = jnp.where(apart, F32(-1e30), F32(0.0))
    for r in range(2):
        for h in range(HEADS):
            value = bias_v[r, h].astype(F32)
            biasf[r, h // 2, WT * (h % 2) : WT * (h % 2 + 1), :] = value + penalty if r else value

    lane = lax.broadcasted_iota(jnp.int32, (1, 128), 1)
    first = lane < 64
    scale0 = jnp.where(first, F32(0.125), F32(0.0))
    scale1 = jnp.where(first, F32(0.0), F32(0.125))

    def attend(r, x):
        qkv = jnp.dot(x, wqkv[...], preferred_element_type=F32)
        parts = []
        for p in range(HEADS // 2):
            qf = qkv[:, 128 * p : 128 * (p + 1)]
            kp = qkv[:, D + 128 * p : D + 128 * (p + 1)].astype(BF16)
            vp = qkv[:, 2 * D + 128 * p : 2 * D + 128 * (p + 1)].astype(BF16)
            q2 = jnp.concatenate([(qf * scale0).astype(BF16), (qf * scale1).astype(BF16)], 0)
            s = lax.dot_general(q2, kp, (((1,), (1,)), ((), ())), preferred_element_type=F32)
            s = s + biasf[r, p]
            e = jnp.exp(s - jnp.max(s, axis=-1, keepdims=True)).astype(BF16)
            vx = jnp.concatenate([vp, jnp.ones((WT, 128), BF16)], 1)
            o = jnp.dot(e, vx, preferred_element_type=F32)
            num = jnp.where(first, o[:WT, :128], o[WT:, :128])
            den = jnp.where(first, o[:WT, 128:], o[WT:, 128:])
            parts.append((num / den).astype(BF16))
        att = jnp.concatenate(parts, 1)
        proj = jnp.dot(att, wout[...], preferred_element_type=F32) + b_out[...]
        return proj.astype(BF16).astype(F32)

    def token(l, i):
        return WLON * (WLAT * l + i)

    def compute(r, slot):
        x = jnp.concatenate([win_in[slot, t].astype(BF16) for t in range(LT)], 1)
        proj = attend(r, x)
        for t in range(LT):
            win_out[slot, t] = proj[:, 128 * t : 128 * (t + 1)]

    def take(slot, i0, i1, row0, col):
        for l in range(LEV):
            for i in range(i0, i1):
                j = token(l, i)
                win_in[slot, :, j : j + WLON, :] = fx[:, l, row0 + i - i0, col : col + WLON, :]

    def keep(slot, i1, row0, col, own):
        for l in range(LEV):
            for i in range(i1):
                j = token(l, i)
                pf[:, l, row0 + i, col : col + own, :] = win_out[slot, :, j : j + own, :]

    def pack(slot, i0, i1, off, width, dst, n):
        for l in range(LEV):
            for i in range(i0, i1):
                j = token(l, i) + off
                dst[:, n : n + width, :] = win_out[slot, :, j : j + width, :]
                n += width

    def window_m(b):
        slot = b % 2
        col = SLON + WLON * b
        take(slot, 0, WLAT, 3, col)
        compute(0, slot)
        keep(slot, WLAT, 3, col, WLON if b < 3 else SLON)
        if b == 3:
            pack(slot, 0, WLAT, SLON, SLON, cmp_f.at[0], 0)
            narrow(cmp_f.at[0], s80.at[1], 0, 80)
            wm.start()

    def window_s(b):
        slot = b % 2
        col = SLON + WLON * b
        take(slot, 0, SLAT, 9, col)
        for l in range(LEV):
            j = token(l, SLAT)
            if b < 3:
                n = X_WINDOW + 72 * b + 36 * l
                win_in[slot, :, j : j + 36, :] = stage[:, n : n + 36, :]
            else:
                for i in range(SLAT):
                    n = SLON * (SLAT * l + i)
                    jj = j + WLON * i
                    win_in[slot, :, jj : jj + SLON, :] = stage[
                        :, X_CORNER_E + n : X_CORNER_E + n + SLON, :
                    ]
                    win_in[slot, :, jj + SLON : jj + WLON, :] = cmp_f[1, :, n : n + SLON, :]
        compute(1, slot)
        if b == 3:
            pack(slot, SLAT, WLAT, 0, SLON, stage_r, 0)
            narrow(stage_r, rs, *R_CUTS[0][::2])
            r_send(0)
            pack(slot, SLAT, WLAT, SLON, SLON, cmp_f.at[0], 0)
            narrow(cmp_f.at[0], s48.at[2], 0, 48)
            diag.start()
            pack(slot, 0, SLAT, SLON, SLON, cmp_f.at[1], 0)
            narrow(cmp_f.at[1], s48.at[1], 0, 48)
            ws.start()
        else:
            for l in range(LEV):
                n, j = R_WINDOW + 72 * b + 36 * l, token(l, SLAT)
                stage_r[:, n : n + 36, :] = win_out[slot, :, j : j + 36, :]
            narrow(stage_r, rs, *R_CUTS[b + 1][::2])
            r_send(b + 1)
        keep(slot, SLAT, 9, col, WLON if b < 3 else SLON)

    loads[C_WQKV].wait()
    loads[C_WOUT].wait()
    loads[C_B].wait()
    for b in range(3):
        window_m(b)

    pl.when(inner)(lambda: pl.semaphore_wait(barrier, 6))
    pl.when(jnp.logical_not(inner))(lambda: pl.semaphore_wait(barrier, 9))
    for k in range(4):
        x_send(k)
    em.start()
    es.start()
    x_relay(0)
    x_relay(1)
    em.wait_recv()
    widen(r80.at[0], cmp_f.at[0], 0, 80)
    n = 0
    for l in range(LEV):
        for row in range(3, 9):
            fx[:, l, row, 48 : 48 + SLON, :] = cmp_f[0, :, n : n + SLON, :]
            n += SLON
    window_m(3)
    x_relay(2)
    x_relay(3)

    def x_take(k):
        x_direct(k).wait_recv()
        x_other(k).wait_recv()
        if k == 0:
            corner.start()
        widen(xr, stage, *X_CUTS[k][::2])

    x_take(0)
    es.wait_recv()
    widen(r48.at[0], cmp_f.at[0], 0, 48)
    n = 0
    for l in range(LEV):
        for row in range(9, 12):
            fx[:, l, row, 48 : 48 + SLON, :] = cmp_f[0, :, n : n + SLON, :]
            n += SLON
    corner.wait_recv()
    widen(cor, cmp_f.at[1], 0, 48)
    window_s(3)
    for b in range(3):
        x_take(b + 1)
        window_s(b)
    r_relay(0)

    loads[C_G].wait()
    loads[C_H].wait()

    def finish(row0, row1):
        for l in range(LEV):
            for row in range(row0, row1):
                v = jnp.concatenate([pf[t, l, row] for t in range(LT)], 1)
                mean = jnp.mean(v, axis=-1, keepdims=True)
                d = v - mean
                var = jnp.mean(d * d, axis=-1, keepdims=True)
                normed = d * lax.rsqrt(var + F32(1e-5)) * gain[...] + shift[...]
                out_v[l, row] = (lat_v[l, row].astype(F32) + normed).astype(BF16)

    def place_rows(src, n, width, row0, count, col):
        for l in range(LEV):
            for i in range(count):
                pf[:, l, row0 + i, col : col + width, :] = src[:, n : n + width, :]
                n += width

    wm.wait_recv()
    widen(r80.at[1], cmp_f.at[0], 0, 80)
    place_rows(cmp_f.at[0], 0, SLON, 3, WLAT, 0)
    finish(3, 9)
    r_relay(1)
    ws.wait_recv()
    widen(r48.at[1], cmp_f.at[1], 0, 48)
    place_rows(cmp_f.at[1], 0, SLON, 9, SLAT, 0)
    finish(9, 12)
    r_relay(2)
    r_relay(3)
    diag.wait_recv()
    widen(r48.at[2], cmp_f.at[1], 0, 48)
    place_rows(cmp_f.at[1], 0, SLON, 0, SLAT, 0)
    groups = [(36 * l + WLON * i + 72 * b + R_WINDOW, WLON, l, i, SLON + WLON * b)
              for b in range(3) for l in range(LEV) for i in range(SLAT)]
    groups += [(SLON * (SLAT * l + i), SLON, l, i, 42) for l in range(LEV) for i in range(SLAT)]
    for k in range(4):
        r_direct(k).wait_recv()
        r_other(k).wait_recv()
        a, _, b = R_CUTS[k]
        widen(rr, stage, a, b)
        for n, width, l, i, col in groups:
            if a < n + width <= b:
                pf[:, l, i, col : col + width, :] = stage[:, n : n + width, :]
    finish(0, 3)

    for copy in (em, es, corner, wm, ws, diag):
        copy.wait_send()
    for k in range(4):
        x_direct(k).wait_send()
        x_other(k).wait_send()
        r_direct(k).wait_send()
        r_other(k).wait_send()
        pl.when(tail)(x_forward(k).wait_send)
        pl.when(head)(r_forward(k).wait_send)


def local_step(nlat, nlon, latent, w_qkv, w_out, b_out, norm_gain, norm_shift, earth_bias):
    hbm = pl.BlockSpec(memory_space=pl.ANY)
    tile = latent.shape
    return pl.pallas_call(
        functools.partial(kernel, nlat, nlon),
        out_shape=pltpu.VMEM(tile, BF16),
        in_specs=[hbm] * 7,
        out_specs=pl.BlockSpec(memory_space=pltpu.VMEM),
        scratch_shapes=[
            pltpu.VMEM(tile, BF16),
            pltpu.VMEM((D, 3 * D), BF16),
            pltpu.VMEM((D, D), BF16),
            pltpu.VMEM((1, D), F32),
            pltpu.VMEM((1, D), F32),
            pltpu.VMEM((1, D), F32),
            pltpu.VMEM((2, HEADS, WT, WT), BF16),
            pltpu.VMEM((2, HEADS // 2, 2 * WT, WT), F32),
            pltpu.VMEM((LT, LEV, 12, 64, 128), F32),
            pltpu.VMEM((LT, LEV, 12, 48, 128), F32),
            pltpu.VMEM((2, LT, WT, 128), F32),
            pltpu.VMEM((2, LT, WT, 128), F32),
            pltpu.VMEM((LT, 288, 128), F32),
            pltpu.VMEM((LT, 256, 128), F32),
            pltpu.VMEM((288, D), BF16),
            pltpu.VMEM((288, D), BF16),
            pltpu.VMEM((288, D), BF16),
            pltpu.VMEM((256, D), BF16),
            pltpu.VMEM((256, D), BF16),
            pltpu.VMEM((256, D), BF16),
            pltpu.VMEM((2, LT, 80, 128), F32),
            pltpu.VMEM((2, 80, D), BF16),
            pltpu.VMEM((3, 48, D), BF16),
            pltpu.VMEM((2, 80, D), BF16),
            pltpu.VMEM((3, 48, D), BF16),
            pltpu.VMEM((48, D), BF16),
            pltpu.SemaphoreType.DMA((9,)),
            pltpu.SemaphoreType.DMA((COPIES,)),
            pltpu.SemaphoreType.DMA((COPIES,)),
        ],
        compiler_params=pltpu.CompilerParams(
            collective_id=0, has_side_effects=True, vmem_limit_bytes=60 * 1024 * 1024
        ),
        name="swin_window_attention",
    )(
        latent, w_qkv, w_out, b_out.reshape(1, D), norm_gain.reshape(1, D),
        norm_shift.reshape(1, D), earth_bias,
    )


def solution(mesh):
    placed = (P(None, "lat", "lon", None), P(), P(), P(), P(), P(), P("lat", None, None, None))
    step = functools.partial(local_step, mesh.shape["lat"], mesh.shape["lon"])
    return jax.shard_map(
        step, mesh=mesh, in_specs=placed, out_specs=P(None, "lat", "lon", None), check_vma=False
    )
```

```python
import functools

import jax
import jax.numpy as jnp
from jax import lax
from jax.experimental import pallas as pl
from jax.experimental.pallas import tpu as pltpu
from jax.sharding import PartitionSpec as P

LEV = 2
WLAT = 6
WLON = 12
SLAT = 3
SLON = 6
WT = 144
HEADS = 8
D = 512
LT = 4
GROUP = 4
F32 = jnp.float32
BF16 = jnp.bfloat16
MESH = pl.DeviceIdType.MESH

(C_N, C_M, C_S, C_WQKV, C_WOUT, C_BIAS, C_B, C_G, C_H) = range(9)
XA, XB, XR, XF, RA, RB, RR, RF = range(0, 32, 4)
BA, BP, EM, ES, EN, COR, CORN, WM, WS, WN, DIAG = range(32, 43)
COPIES = 43

X_CUTS = ((0, 48, 80), (80, 128, 160), (160, 192, 224), (224, 256, 288))
T_CUTS = ((0, 32, 80), (80, 112, 160), (160, 176, 224), (224, 240, 288))
X_CORNER_E = 36
X_WINDOW = 72
R_CUTS = ((0, 64), (64, 144), (144, 208), (208, 256))
R_CORNER = 216
B_ROWS = 336
HALF = WT // 2


def kernel(
    nlat, nlon,
    lat_h, wqkv_h, wout_h, b_h, gain_h, shift_h, bias_h, out_v,
    lat_v, wqkv, wout, b_out, gain, shift, bias_v, biasf, fx, pf, win_in, win_out,
    stage, stage_n, stage_r, xs, xr, xrelay, rs, rr, rrelay, bt, bstage, bs, br, bp,
    cmp_f, s80, s48, r80, r48, cor, corn,
    lsem, ssem, rsem,
):
    ilat, ilon = lax.axis_index("lat"), lax.axis_index("lon")

    def at(dlat, dlon):
        return {
            "lat": lax.rem(ilat + dlat + nlat, nlat),
            "lon": lax.rem(ilon + dlon + nlon, nlon),
        }

    core = lax.rem(ilon, 2)
    place = lax.rem(ilat, GROUP)
    head, tail = place == 0, place == GROUP - 1
    inner = jnp.logical_and(place != 0, place != GROUP - 1)
    not_head, not_tail = jnp.logical_not(head), jnp.logical_not(tail)
    late_send = ilat == 0
    early_send = jnp.logical_not(late_send)
    forward_first = jnp.logical_and(head, early_send)
    forward_last = late_send

    barrier = pltpu.get_barrier_semaphore()

    def greet(who):
        pl.semaphore_signal(barrier, inc=1, device_id=who, device_id_type=MESH)

    for who in (at(-1, 0), at(1, 0), at(0, -1), at(0, 1), at(-1, -1), at(1, 1)):
        greet(who)

    @pl.when(head)
    def _():
        for who in (at(GROUP - 1, 0), at(GROUP, 0), at(-GROUP, 0)):
            greet(who)

    @pl.when(tail)
    def _():
        for who in (at(1 - GROUP, 0), at(GROUP, 0), at(-GROUP, 0)):
            greet(who)

    def local(src, dst, which):
        return pltpu.make_async_copy(src, dst, lsem.at[which])

    def remote(src, dst, which, who, send=None):
        return pltpu.make_async_remote_copy(
            src_ref=src, dst_ref=dst, send_sem=ssem.at[which if send is None else send],
            recv_sem=rsem.at[which], device_id=who, device_id_type=MESH,
        )

    loads = {
        C_S: local(lat_h.at[:, 9:12], lat_v.at[:, 9:12], C_S),
        C_N: local(lat_h.at[:, 0:3], lat_v.at[:, 0:3], C_N),
        C_BIAS: local(bias_h, bias_v, C_BIAS),
        C_M: local(lat_h.at[:, 3:9], lat_v.at[:, 3:9], C_M),
        C_WQKV: local(wqkv_h, wqkv, C_WQKV),
        C_WOUT: local(wout_h, wout, C_WOUT),
        C_B: local(b_h, b_out, C_B),
        C_G: local(gain_h, gain, C_G),
        C_H: local(shift_h, shift, C_H),
    }
    for copy in loads.values():
        copy.start()

    def rows(ref, a, b):
        return ref.at[a:b]

    def x_direct(k):
        a, m, _ = X_CUTS[k]
        return remote(rows(xs, a, m), rows(xr, a, m), XA + k, at(-1, 0))

    def x_other(k):
        _, m, b = X_CUTS[k]
        return remote(rows(xs, m, b), rows(xr, m, b), XB + k, at(-1, 0))

    def x_around(k):
        _, m, b = X_CUTS[k]
        return remote(rows(xs, m, b), rows(xrelay, m, b), XR + k, at(GROUP - 1, 0), XB + k)

    def x_forward(k):
        _, m, b = X_CUTS[k]
        return remote(rows(xrelay, m, b), rows(xr, m, b), XB + k, at(-GROUP, 0), XF + k)

    def t_direct(k):
        a, m, _ = T_CUTS[k]
        return remote(rows(rs, a, m), rows(rr, a, m), RA + k, at(1, 0))

    def t_around(k):
        _, m, b = T_CUTS[k]
        return remote(rows(rs, m, b), rows(rrelay, m, b), RR + k, at(1 - GROUP, 0), RB + k)

    def t_forward(k):
        _, m, b = T_CUTS[k]
        return remote(rows(rrelay, m, b), rows(rr, m, b), RB + k, at(GROUP, 0), RF + k)

    b_direct = remote(bs, br, BA, at(1, 0))
    b_pair = remote(br, bp, BP, at(0, 1 - 2 * core))

    def r_copy(k):
        return remote(rows(rs, *R_CUTS[k]), rows(rr, *R_CUTS[k]), RA + k, at(1, 0))

    def x_send(k):
        pl.when(head)(x_around(k).start)
        pl.when(not_head)(x_other(k).start)
        x_direct(k).start()

    def t_send(k):
        t_around(k).start()
        t_direct(k).start()

    def x_relay(k):
        @pl.when(tail)
        def _():
            x_around(k).wait_recv()
            x_forward(k).start()

    def t_relay(k, when):
        @pl.when(when)
        def _():
            t_around(k).wait_recv()
            t_forward(k).start()

    em = remote(s80.at[0], r80.at[0], EM, at(0, -1))
    es = remote(s48.at[0], r48.at[0], ES, at(0, -1))
    en = remote(s48.at[3], r48.at[3], EN, at(0, -1))
    corner = remote(rows(xr, 0, 48), cor, COR, at(0, -1))
    corner_n = remote(rows(rr, 0, 48), corn, CORN, at(0, -1))
    wm = remote(s80.at[1], r80.at[1], WM, at(0, 1))
    ws = remote(s48.at[1], r48.at[1], WS, at(0, 1))
    wn = remote(s48.at[4], r48.at[4], WN, at(0, 1))
    diag = remote(s48.at[2], r48.at[2], DIAG, at(1, 1))

    def widen(src, dst, a, b):
        for t in range(LT):
            dst[t, a:b, :] = src[a:b, 128 * t : 128 * (t + 1)].astype(F32)

    def narrow(src, dst, a, b):
        for t in range(LT):
            dst[a:b, 128 * t : 128 * (t + 1)] = src[t, a:b, :].astype(BF16)

    def spread(row0, row1):
        for l in range(LEV):
            for row in range(row0, row1):
                for t in range(LT):
                    fx[t, l, row, 0:48] = lat_v[l, row, :, 128 * t : 128 * (t + 1)].astype(F32)

    def pack_stream(dst_f, dst, row0):
        n = 0
        for col, width in ((0, 6), (42, 6), (6, 12), (18, 12), (30, 12)):
            for l in range(LEV):
                for i in range(SLAT):
                    dst_f[:, n : n + width, :] = fx[:, l, row0 + i, col : col + width, :]
                    n += width
        narrow(dst_f, dst, 0, 288)

    def pack_west(slot, dst, row0, row1, size):
        n = 0
        for l in range(LEV):
            for row in range(row0, row1):
                cmp_f[slot, :, n : n + SLON, :] = fx[:, l, row, 0:SLON, :]
                n += SLON
        narrow(cmp_f.at[slot], dst, 0, size)

    def unpack_east(src, slot, row0, row1, size):
        widen(src, cmp_f.at[slot], 0, size)
        n = 0
        for l in range(LEV):
            for row in range(row0, row1):
                fx[:, l, row, 48 : 48 + SLON, :] = cmp_f[slot, :, n : n + SLON, :]
                n += SLON

    loads[C_S].wait()
    spread(9, 12)

    @pl.when(tail)
    def _():
        pack_stream(stage_n, rs, 9)
        pl.semaphore_wait(barrier, 9)
        t_send(0)

    pack_west(1, s48.at[0], 9, 12, 48)
    loads[C_BIAS].wait()

    @pl.when(tail)
    def _():
        bt[HEADS] = jnp.concatenate(
            [bias_v[1, h].astype(F32)[:, 128:WT] for h in range(HEADS)], 1
        )
        for g in range(4):
            bt[g] = bias_v[1, 4 * core + g, :, 0:128].astype(F32)
            bstage[HALF * g : HALF * g + 36, :] = bt[g, 36:72, :]
            bstage[HALF * g + 36 : HALF * (g + 1), :] = bt[g, 108:WT, :]
        for c in range(2):
            @pl.when(core == c)
            def _():
                bstage[4 * HALF : 4 * HALF + 36, :] = bt[HEADS, 36 + 72 * c : 72 + 72 * c, :]
        bs[...] = bstage[...].astype(BF16)
        b_direct.start()

    loads[C_N].wait()
    spread(0, 3)
    pack_stream(stage, xs, 0)
    loads[C_M].wait()
    spread(3, 9)
    pack_west(0, s80.at[0], 3, 9, 80)
    pl.when(head)(lambda: pack_west(1, s48.at[3], 0, 3, 48))

    def greet_and_send():
        pl.when(inner)(lambda: pl.semaphore_wait(barrier, 6))
        pl.when(head)(lambda: pl.semaphore_wait(barrier, 9))
        x_send(0)
        em.start()
        es.start()
        pl.when(head)(en.start)
        x_send(1)

    pl.when(early_send)(greet_and_send)

    is_last = ilat == nlat - 1

    def south_half(axis):
        n = lax.broadcasted_iota(jnp.int32, (WT, WT), axis)
        return jnp.logical_or(jnp.logical_and(n >= 36, n < 72), n >= 108)

    apart = jnp.logical_and(south_half(0) != south_half(1), is_last)
    penalty = jnp.where(apart, F32(-1e30), F32(0.0))
    for r in range(2):
        for h in range(HEADS):
            value = bias_v[r, h].astype(F32)
            biasf[r, h // 2, WT * (h % 2) : WT * (h % 2 + 1), :] = value + penalty if r else value

    lane = lax.broadcasted_iota(jnp.int32, (1, 128), 1)
    first = lane < 64
    scale0 = jnp.where(first, F32(0.125), F32(0.0))
    scale1 = jnp.where(first, F32(0.0), F32(0.125))

    def attend(r, x):
        qkv = jnp.dot(x, wqkv[...], preferred_element_type=F32)
        parts = []
        for p in range(HEADS // 2):
            qf = qkv[:, 128 * p : 128 * (p + 1)]
            kp = qkv[:, D + 128 * p : D + 128 * (p + 1)].astype(BF16)
            vp = qkv[:, 2 * D + 128 * p : 2 * D + 128 * (p + 1)].astype(BF16)
            q2 = jnp.concatenate([(qf * scale0).astype(BF16), (qf * scale1).astype(BF16)], 0)
            s = lax.dot_general(q2, kp, (((1,), (1,)), ((), ())), preferred_element_type=F32)
            s = s + biasf[r, p]
            e = jnp.exp(s - jnp.max(s, axis=-1, keepdims=True)).astype(BF16)
            vx = jnp.concatenate([vp, jnp.ones((WT, 128), BF16)], 1)
            o = jnp.dot(e, vx, preferred_element_type=F32)
            num = jnp.where(first, o[:WT, :128], o[WT:, :128])
            den = jnp.where(first, o[:WT, 128:], o[WT:, 128:])
            parts.append((num / den).astype(BF16))
        att = jnp.concatenate(parts, 1)
        proj = jnp.dot(att, wout[...], preferred_element_type=F32) + b_out[...]
        return proj.astype(BF16).astype(F32)

    def token(l, i):
        return WLON * (WLAT * l + i)

    def compute(r, slot):
        x = jnp.concatenate([win_in[slot, t].astype(BF16) for t in range(LT)], 1)
        proj = attend(r, x)
        for t in range(LT):
            win_out[slot, t] = proj[:, 128 * t : 128 * (t + 1)]

    def take(slot, i0, i1, row0, col):
        for l in range(LEV):
            for i in range(i0, i1):
                j = token(l, i)
                win_in[slot, :, j : j + WLON, :] = fx[:, l, row0 + i - i0, col : col + WLON, :]

    def keep(slot, i1, row0, col, own):
        for l in range(LEV):
            for i in range(i1):
                j = token(l, i)
                pf[:, l, row0 + i, col : col + own, :] = win_out[slot, :, j : j + own, :]

    def pack(slot, i0, i1, off, width, dst, n):
        for l in range(LEV):
            for i in range(i0, i1):
                j = token(l, i) + off
                dst[:, n : n + width, :] = win_out[slot, :, j : j + width, :]
                n += width

    def window_m(b):
        slot = b % 2
        col = SLON + WLON * b
        take(slot, 0, WLAT, 3, col)
        compute(0, slot)
        keep(slot, WLAT, 3, col, WLON if b < 3 else SLON)
        if b == 3:
            pack(slot, 0, WLAT, SLON, SLON, cmp_f.at[0], 0)
            narrow(cmp_f.at[0], s80.at[1], 0, 80)
            wm.start()

    def window_s(b):
        slot = b % 2
        col = SLON + WLON * b
        take(slot, 0, SLAT, 9, col)
        for l in range(LEV):
            j = token(l, SLAT)
            if b < 3:
                n = X_WINDOW + 72 * b + 36 * l
                win_in[slot, :, j : j + 36, :] = stage[:, n : n + 36, :]
            else:
                for i in range(SLAT):
                    n = SLON * (SLAT * l + i)
                    jj = j + WLON * i
                    win_in[slot, :, jj : jj + SLON, :] = stage[
                        :, X_CORNER_E + n : X_CORNER_E + n + SLON, :
                    ]
                    win_in[slot, :, jj + SLON : jj + WLON, :] = cmp_f[1, :, n : n + SLON, :]
        compute(1, slot)

        @pl.when(not_tail)
        def _():
            if b == 3:
                pack(slot, SLAT, WLAT, 0, SLON, stage_r, R_CORNER)
            else:
                for l in range(LEV):
                    n, j = 72 * b + 36 * l, token(l, SLAT)
                    stage_r[:, n : n + 36, :] = win_out[slot, :, j : j + 36, :]
            narrow(stage_r, rs, *R_CUTS[b])
            if b == 3:
                r_copy(b).start()
                pack(slot, SLAT, WLAT, SLON, SLON, cmp_f.at[0], 0)
                narrow(cmp_f.at[0], s48.at[2], 0, 48)
                diag.start()
            elif b == 2:
                r_copy(b).start()
            else:
                pl.when(early_send)(r_copy(b).start)

        if b == 3:
            pack(slot, 0, SLAT, SLON, SLON, cmp_f.at[1], 0)
            narrow(cmp_f.at[1], s48.at[1], 0, 48)
            ws.start()
        keep(slot, SLAT, 9, col, WLON if b < 3 else SLON)

    def window_n(b):
        slot = b % 2
        col = SLON + WLON * b
        for l in range(LEV):
            for i in range(SLAT):
                j = token(l, SLAT + i)
                win_in[slot, :, j : j + WLON, :] = fx[:, l, i, col : col + WLON, :]
            j = token(l, 0)
            if b < 3:
                n = X_WINDOW + 72 * b + 36 * l
                win_in[slot, :, j : j + 36, :] = stage_n[:, n : n + 36, :]
            else:
                for i in range(SLAT):
                    n = SLON * (SLAT * l + i)
                    jj = j + WLON * i
                    win_in[slot, :, jj : jj + SLON, :] = stage_n[
                        :, X_CORNER_E + n : X_CORNER_E + n + SLON, :
                    ]
                    win_in[slot, :, jj + SLON : jj + WLON, :] = cmp_f[1, :, n : n + SLON, :]
        compute(2, slot)
        own = WLON if b < 3 else SLON
        for l in range(LEV):
            for i in range(SLAT):
                j = token(l, SLAT + i)
                pf[:, l, i, col : col + own, :] = win_out[slot, :, j : j + own, :]
        if b == 3:
            pack(slot, SLAT, WLAT, SLON, SLON, cmp_f.at[0], 0)
            narrow(cmp_f.at[0], s48.at[4], 0, 48)
            wn.start()

    loads[C_WQKV].wait()
    loads[C_WOUT].wait()
    loads[C_B].wait()
    def x_take(k):
        x_direct(k).wait_recv()
        x_other(k).wait_recv()
        widen(xr, stage, *X_CUTS[k][::2])

    def last_of_first_band():
        em.wait_recv()
        unpack_east(r80.at[0], 0, 3, 9, 80)
        window_m(3)

    def step_of_sends(k):
        pl.when(early_send)(lambda: x_send(k))

    window_m(0)
    step_of_sends(2)
    window_m(1)
    pl.when(tail)(lambda: t_send(1))
    step_of_sends(3)
    x_relay(0)
    window_m(2)
    pl.when(tail)(lambda: t_send(2))
    x_relay(1)
    pl.when(early_send)(last_of_first_band)
    pl.when(tail)(lambda: t_send(3))
    x_relay(2)
    x_relay(3)
    t_relay(0, forward_first)

    x_take(0)
    pl.when(early_send)(corner.start)
    x_take(1)
    window_s(0)
    t_relay(1, forward_first)
    x_take(2)
    window_s(1)
    t_relay(2, forward_first)
    @pl.when(late_send)
    def _():
        greet_and_send()
        corner.start()
        r_copy(0).start()
        r_copy(1).start()
        x_send(2)
        x_send(3)

    x_take(3)
    window_s(2)
    t_relay(3, forward_first)
    pl.when(late_send)(last_of_first_band)
    es.wait_recv()
    unpack_east(r48.at[0], 0, 9, 12, 48)
    corner.wait_recv()
    widen(cor, cmp_f.at[1], 0, 48)
    window_s(3)
    t_relay(0, forward_last)

    loads[C_G].wait()
    loads[C_H].wait()

    def finish(row0, row1):
        for l in range(LEV):
            for row in range(row0, row1):
                v = jnp.concatenate([pf[t, l, row] for t in range(LT)], 1)
                mean = jnp.mean(v, axis=-1, keepdims=True)
                d = v - mean
                var = jnp.mean(d * d, axis=-1, keepdims=True)
                normed = d * lax.rsqrt(var + F32(1e-5)) * gain[...] + shift[...]
                out_v[l, row] = (lat_v[l, row].astype(F32) + normed).astype(BF16)

    def place_rows(src, n, width, row0, count, col):
        for l in range(LEV):
            for i in range(count):
                pf[:, l, row0 + i, col : col + width, :] = src[:, n : n + width, :]
                n += width

    def finish_own():
        wm.wait_recv()
        widen(r80.at[1], cmp_f.at[0], 0, 80)
        place_rows(cmp_f.at[0], 0, SLON, 3, WLAT, 0)
        finish(3, 9)
        ws.wait_recv()
        widen(r48.at[1], cmp_f.at[0], 0, 48)
        place_rows(cmp_f.at[0], 0, SLON, 9, SLAT, 0)
        finish(9, 12)

    pl.when(not_head)(finish_own)

    @pl.when(not_head)
    def _():
        diag.wait_recv()
        widen(r48.at[2], cmp_f.at[1], 0, 48)
        place_rows(cmp_f.at[1], 0, SLON, 0, SLAT, 0)
        groups = [(36 * l + WLON * i + 72 * b, WLON, l, i, SLON + WLON * b)
                  for b in range(3) for l in range(LEV) for i in range(SLAT)]
        groups += [(R_CORNER + SLON * (SLAT * l + i), SLON, l, i, 42) for l in range(LEV) for i in range(SLAT)]
        for k in range(4):
            r_copy(k).wait_recv()
            a, b = R_CUTS[k]
            widen(rr, stage, a, b)
            for n, width, l, i, col in groups:
                if a < n + width <= b:
                    pf[:, l, i, col : col + width, :] = stage[:, n : n + width, :]

    @pl.when(head)
    def _():
        def t_take(k):
            t_direct(k).wait_recv()
            t_forward(k).wait_recv()
            if k == 0:
                corner_n.start()
            widen(rr, stage_n, *X_CUTS[k][::2])

        b_direct.wait_recv()
        b_pair.start()
        t_take(0)
        t_relay(1, forward_last)
        b_pair.wait_recv()
        for g in range(HEADS + 1):
            bt[g] = jnp.zeros((WT, 128), F32)
        for src, side in ((br, core), (bp, 1 - core)):
            bstage[...] = src[...].astype(F32)
            for g in range(4):
                bt[4 * side + g, 36:72, :] = bstage[HALF * g : HALF * g + 36, :]
                bt[4 * side + g, 108:WT, :] = bstage[HALF * g + 36 : HALF * (g + 1), :]
            for c in range(2):
                @pl.when(side == c)
                def _():
                    bt[HEADS, 36 + 72 * c : 72 + 72 * c, :] = bstage[4 * HALF : 4 * HALF + 36, :]
        at_pole = jnp.logical_and(south_half(0) != south_half(1), ilat == 0)
        pole = jnp.where(at_pole, F32(-1e30), F32(0.0))
        for h in range(HEADS):
            rest = bt[HEADS][:, 16 * h : 16 * (h + 1)]
            biasf[2, h // 2, WT * (h % 2) : WT * (h % 2 + 1), :] = (
                jnp.concatenate([bt[h], rest], 1) + pole
            )
        en.wait_recv()
        unpack_east(r48.at[3], 0, 0, 3, 48)
        corner_n.wait_recv()
        widen(corn, cmp_f.at[1], 0, 48)
        t_relay(2, forward_last)
        t_relay(3, forward_last)
        window_n(3)
        finish_own()
        for b in range(3):
            t_take(b + 1)
            window_n(b)
        wn.wait_recv()
        widen(r48.at[4], cmp_f.at[1], 0, 48)
        place_rows(cmp_f.at[1], 0, SLON, 0, SLAT, 0)

    finish(0, 3)

    for copy in (em, es, corner, wm, ws):
        copy.wait_send()
    for k in range(4):
        x_direct(k).wait_send()
        x_other(k).wait_send()

    @pl.when(not_tail)
    def _():
        diag.wait_send()
        for k in range(4):
            r_copy(k).wait_send()

    @pl.when(tail)
    def _():
        b_direct.wait_send()
        for k in range(4):
            x_forward(k).wait_send()
            t_direct(k).wait_send()
            t_around(k).wait_send()

    @pl.when(head)
    def _():
        for copy in (en, wn, corner_n, b_pair):
            copy.wait_send()
        for k in range(4):
            t_forward(k).wait_send()


def local_step(nlat, nlon, latent, w_qkv, w_out, b_out, norm_gain, norm_shift, earth_bias):
    hbm = pl.BlockSpec(memory_space=pl.ANY)
    tile = latent.shape
    return pl.pallas_call(
        functools.partial(kernel, nlat, nlon),
        out_shape=pltpu.VMEM(tile, BF16),
        in_specs=[hbm] * 7,
        out_specs=pl.BlockSpec(memory_space=pltpu.VMEM),
        scratch_shapes=[
            pltpu.VMEM(tile, BF16),
            pltpu.VMEM((D, 3 * D), BF16),
            pltpu.VMEM((D, D), BF16),
            pltpu.VMEM((1, D), F32),
            pltpu.VMEM((1, D), F32),
            pltpu.VMEM((1, D), F32),
            pltpu.VMEM((2, HEADS, WT, WT), BF16),
            pltpu.VMEM((3, HEADS // 2, 2 * WT, WT), F32),
            pltpu.VMEM((LT, LEV, 12, 64, 128), F32),
            pltpu.VMEM((LT, LEV, 12, 48, 128), F32),
            pltpu.VMEM((2, LT, WT, 128), F32),
            pltpu.VMEM((2, LT, WT, 128), F32),
            pltpu.VMEM((LT, 288, 128), F32),
            pltpu.VMEM((LT, 288, 128), F32),
            pltpu.VMEM((LT, 256, 128), F32),
            pltpu.VMEM((288, D), BF16),
            pltpu.VMEM((288, D), BF16),
            pltpu.VMEM((288, D), BF16),
            pltpu.VMEM((288, D), BF16),
            pltpu.VMEM((288, D), BF16),
            pltpu.VMEM((288, D), BF16),
            pltpu.VMEM((HEADS + 1, WT, 128), F32),
            pltpu.VMEM((B_ROWS, 128), F32),
            pltpu.VMEM((B_ROWS, 128), BF16),
            pltpu.VMEM((B_ROWS, 128), BF16),
            pltpu.VMEM((B_ROWS, 128), BF16),
            pltpu.VMEM((2, LT, 80, 128), F32),
            pltpu.VMEM((2, 80, D), BF16),
            pltpu.VMEM((5, 48, D), BF16),
            pltpu.VMEM((2, 80, D), BF16),
            pltpu.VMEM((5, 48, D), BF16),
            pltpu.VMEM((48, D), BF16),
            pltpu.VMEM((48, D), BF16),
            pltpu.SemaphoreType.DMA((9,)),
            pltpu.SemaphoreType.DMA((COPIES,)),
            pltpu.SemaphoreType.DMA((COPIES,)),
        ],
        compiler_params=pltpu.CompilerParams(
            collective_id=0, has_side_effects=True, vmem_limit_bytes=60 * 1024 * 1024
        ),
        name="swin_window_attention",
    )(
        latent, w_qkv, w_out, b_out.reshape(1, D), norm_gain.reshape(1, D),
        norm_shift.reshape(1, D), earth_bias,
    )


def solution(mesh):
    placed = (P(None, "lat", "lon", None), P(), P(), P(), P(), P(), P("lat", None, None, None))
    step = functools.partial(local_step, mesh.shape["lat"], mesh.shape["lon"])
    return jax.shard_map(
        step, mesh=mesh, in_specs=placed, out_specs=P(None, "lat", "lon", None), check_vma=False
    )
```

```python
import functools

import jax
import jax.numpy as jnp
from jax import lax
from jax.experimental import pallas as pl
from jax.experimental.pallas import tpu as pltpu
from jax.sharding import PartitionSpec as P

LEV = 2
WLAT = 6
WLON = 12
SLAT = 3
SLON = 6
WT = 144
HEADS = 8
D = 512
LT = 4
GROUP = 4
F32 = jnp.float32
BF16 = jnp.bfloat16
MESH = pl.DeviceIdType.MESH

(C_N, C_M, C_S, C_WQKV, C_WOUT, C_BIAS, C_B, C_G, C_H) = range(9)
XA, XB, XR, XF, RA, RB, RR, RF = range(0, 32, 4)
BA, BP, EM, ES, EN, COR, CORN, WM, WS, WN, DIAG = range(32, 43)
COPIES = 43

X_CUTS = ((0, 48, 80), (80, 128, 160), (160, 192, 224), (224, 256, 288))
T_CUTS = ((0, 32, 80), (80, 112, 160), (160, 176, 224), (224, 240, 288))
X_CORNER_E = 36
X_WINDOW = 72
R_CUTS = ((0, 64), (64, 144), (144, 208), (208, 256))
R_CORNER = 216
B_ROWS = 336
HALF = WT // 2
HALF_ROWS = 80


def kernel(
    nlat, nlon,
    lat_h, wqkv_h, wout_h, b_h, gain_h, shift_h, bias_h, out_v,
    lat_v, wqkv, wout, b_out, gain, shift, bias_v, biasf, bias_n, fx, pf, win_in, win_q, win_out,
    stage, stage_n, stage_r, xs, xr, xrelay, rs, rr, rrelay, bt, bstage, bs, br, bp,
    cmp_f, s80, s48, r80, r48, cor, corn,
    lsem, ssem, rsem,
):
    ilat, ilon = lax.axis_index("lat"), lax.axis_index("lon")

    def at(dlat, dlon):
        return {
            "lat": lax.rem(ilat + dlat + nlat, nlat),
            "lon": lax.rem(ilon + dlon + nlon, nlon),
        }

    core = lax.rem(ilon, 2)
    place = lax.rem(ilat, GROUP)
    head, tail = place == 0, place == GROUP - 1
    inner = jnp.logical_and(place != 0, place != GROUP - 1)
    not_head, not_tail = jnp.logical_not(head), jnp.logical_not(tail)
    late_send = ilat == 0
    early_send = jnp.logical_not(late_send)
    forward_first = jnp.logical_and(head, early_send)
    forward_last = late_send

    barrier = pltpu.get_barrier_semaphore()

    def greet(who):
        pl.semaphore_signal(barrier, inc=1, device_id=who, device_id_type=MESH)

    for who in (at(-1, 0), at(1, 0), at(0, -1), at(0, 1), at(-1, -1), at(1, 1)):
        greet(who)

    @pl.when(head)
    def _():
        for who in (at(GROUP - 1, 0), at(GROUP, 0), at(-GROUP, 0)):
            greet(who)

    @pl.when(tail)
    def _():
        for who in (at(1 - GROUP, 0), at(GROUP, 0), at(-GROUP, 0)):
            greet(who)

    def local(src, dst, which):
        return pltpu.make_async_copy(src, dst, lsem.at[which])

    def remote(src, dst, which, who, send=None):
        return pltpu.make_async_remote_copy(
            src_ref=src, dst_ref=dst, send_sem=ssem.at[which if send is None else send],
            recv_sem=rsem.at[which], device_id=who, device_id_type=MESH,
        )

    loads = {
        C_S: local(lat_h.at[:, 9:12], lat_v.at[:, 9:12], C_S),
        C_N: local(lat_h.at[:, 0:3], lat_v.at[:, 0:3], C_N),
        C_BIAS: local(bias_h, bias_v, C_BIAS),
        C_M: local(lat_h.at[:, 3:9], lat_v.at[:, 3:9], C_M),
        C_WQKV: local(wqkv_h, wqkv, C_WQKV),
        C_WOUT: local(wout_h, wout, C_WOUT),
        C_B: local(b_h, b_out, C_B),
        C_G: local(gain_h, gain, C_G),
        C_H: local(shift_h, shift, C_H),
    }
    for copy in loads.values():
        copy.start()

    def rows(ref, a, b):
        return ref.at[a:b]

    def x_direct(k):
        a, m, _ = X_CUTS[k]
        return remote(rows(xs, a, m), rows(xr, a, m), XA + k, at(-1, 0))

    def x_other(k):
        _, m, b = X_CUTS[k]
        return remote(rows(xs, m, b), rows(xr, m, b), XB + k, at(-1, 0))

    def x_around(k):
        _, m, b = X_CUTS[k]
        return remote(rows(xs, m, b), rows(xrelay, m, b), XR + k, at(GROUP - 1, 0), XB + k)

    def x_forward(k):
        _, m, b = X_CUTS[k]
        return remote(rows(xrelay, m, b), rows(xr, m, b), XB + k, at(-GROUP, 0), XF + k)

    def t_direct(k):
        a, m, _ = T_CUTS[k]
        return remote(rows(rs, a, m), rows(rr, a, m), RA + k, at(1, 0))

    def t_around(k):
        _, m, b = T_CUTS[k]
        return remote(rows(rs, m, b), rows(rrelay, m, b), RR + k, at(1 - GROUP, 0), RB + k)

    def t_forward(k):
        _, m, b = T_CUTS[k]
        return remote(rows(rrelay, m, b), rows(rr, m, b), RB + k, at(GROUP, 0), RF + k)

    b_direct = remote(bs, br, BA, at(1, 0))
    b_pair = remote(br, bp, BP, at(0, 1 - 2 * core))

    def r_copy(k):
        return remote(rows(rs, *R_CUTS[k]), rows(rr, *R_CUTS[k]), RA + k, at(1, 0))

    def x_send(k):
        pl.when(head)(x_around(k).start)
        pl.when(not_head)(x_other(k).start)
        x_direct(k).start()

    def t_send(k):
        t_around(k).start()
        t_direct(k).start()

    def x_relay(k):
        @pl.when(tail)
        def _():
            x_around(k).wait_recv()
            x_forward(k).start()

    def t_relay(k, when):
        @pl.when(when)
        def _():
            t_around(k).wait_recv()
            t_forward(k).start()

    em = remote(s80.at[0], r80.at[0], EM, at(0, -1))
    es = remote(s48.at[0], r48.at[0], ES, at(0, -1))
    en = remote(s48.at[3], r48.at[3], EN, at(0, -1))
    corner = remote(rows(xr, 0, 48), cor, COR, at(0, -1))
    corner_n = remote(rows(rr, 0, 48), corn, CORN, at(0, -1))
    wm = remote(s80.at[1], r80.at[1], WM, at(0, 1))
    ws = remote(s48.at[1], r48.at[1], WS, at(0, 1))
    wn = remote(s48.at[4], r48.at[4], WN, at(0, 1))
    diag = remote(s48.at[2], r48.at[2], DIAG, at(1, 1))

    def widen(src, dst, a, b):
        for t in range(LT):
            dst[t, a:b, :] = src[a:b, 128 * t : 128 * (t + 1)].astype(F32)

    def narrow(src, dst, a, b):
        for t in range(LT):
            dst[a:b, 128 * t : 128 * (t + 1)] = src[t, a:b, :].astype(BF16)

    def spread(row0, row1):
        for l in range(LEV):
            for row in range(row0, row1):
                for t in range(LT):
                    fx[t, l, row, 0:48] = lat_v[l, row, :, 128 * t : 128 * (t + 1)].astype(F32)

    def pack_stream(dst_f, dst, row0):
        n = 0
        for col, width in ((0, 6), (42, 6), (6, 12), (18, 12), (30, 12)):
            for l in range(LEV):
                for i in range(SLAT):
                    dst_f[:, n : n + width, :] = fx[:, l, row0 + i, col : col + width, :]
                    n += width
        narrow(dst_f, dst, 0, 288)

    def pack_west(slot, dst, row0, row1, size):
        n = 0
        for l in range(LEV):
            for row in range(row0, row1):
                cmp_f[slot, :, n : n + SLON, :] = fx[:, l, row, 0:SLON, :]
                n += SLON
        narrow(cmp_f.at[slot], dst, 0, size)

    def unpack_east(src, slot, row0, row1, size):
        widen(src, cmp_f.at[slot], 0, size)
        n = 0
        for l in range(LEV):
            for row in range(row0, row1):
                fx[:, l, row, 48 : 48 + SLON, :] = cmp_f[slot, :, n : n + SLON, :]
                n += SLON

    loads[C_S].wait()
    spread(9, 12)

    @pl.when(tail)
    def _():
        pack_stream(stage_n, rs, 9)
        pl.semaphore_wait(barrier, 9)
        t_send(0)

    pack_west(1, s48.at[0], 9, 12, 48)
    loads[C_BIAS].wait()

    @pl.when(tail)
    def _():
        bt[HEADS] = jnp.concatenate(
            [bias_v[1, h].astype(F32)[:, 128:WT] for h in range(HEADS)], 1
        )
        for g in range(4):
            bt[g] = bias_v[1, 4 * core + g, :, 0:128].astype(F32)
            bstage[HALF * g : HALF * g + 36, :] = bt[g, 36:72, :]
            bstage[HALF * g + 36 : HALF * (g + 1), :] = bt[g, 108:WT, :]
        for c in range(2):
            @pl.when(core == c)
            def _():
                bstage[4 * HALF : 4 * HALF + 36, :] = bt[HEADS, 36 + 72 * c : 72 + 72 * c, :]
        bs[...] = bstage[...].astype(BF16)
        b_direct.start()

    loads[C_N].wait()
    spread(0, 3)
    pack_stream(stage, xs, 0)
    loads[C_M].wait()
    spread(3, 9)
    pack_west(0, s80.at[0], 3, 9, 80)
    pl.when(head)(lambda: pack_west(1, s48.at[3], 0, 3, 48))

    def greet_and_send():
        pl.when(inner)(lambda: pl.semaphore_wait(barrier, 6))
        pl.when(head)(lambda: pl.semaphore_wait(barrier, 9))
        em.start()
        es.start()
        pl.when(head)(en.start)
        x_send(0)
        x_send(1)

    pl.when(early_send)(greet_and_send)

    is_last = ilat == nlat - 1

    def south_half(axis):
        n = lax.broadcasted_iota(jnp.int32, (WT, WT), axis)
        return jnp.logical_or(jnp.logical_and(n >= 36, n < 72), n >= 108)

    apart = jnp.logical_and(south_half(0) != south_half(1), is_last)
    penalty = jnp.where(apart, F32(-1e30), F32(0.0))
    for r in range(2):
        for h in range(HEADS):
            value = bias_v[r, h].astype(F32)
            biasf[r, h // 2, WT * (h % 2) : WT * (h % 2 + 1), :] = value + penalty if r else value

    lane = lax.broadcasted_iota(jnp.int32, (1, 128), 1)
    first = lane < 64
    scale0 = jnp.where(first, F32(0.125), F32(0.0))
    scale1 = jnp.where(first, F32(0.0), F32(0.125))

    def attend(bias, x, queries=None):
        if queries is None:
            size = WT
            qkv = jnp.dot(x, wqkv[...], preferred_element_type=F32)
            q, kv = qkv[:, :D], qkv[:, D:]
        else:
            size = queries.shape[0]
            q = jnp.dot(queries, wqkv[:, :D], preferred_element_type=F32)
            kv = jnp.dot(x, wqkv[:, D:], preferred_element_type=F32)
        parts = []
        for p in range(HEADS // 2):
            qf = q[:, 128 * p : 128 * (p + 1)]
            kp = kv[:, 128 * p : 128 * (p + 1)].astype(BF16)
            vp = kv[:, D + 128 * p : D + 128 * (p + 1)].astype(BF16)
            q2 = jnp.concatenate([(qf * scale0).astype(BF16), (qf * scale1).astype(BF16)], 0)
            s = lax.dot_general(q2, kp, (((1,), (1,)), ((), ())), preferred_element_type=F32)
            s = s + bias[p]
            e = jnp.exp(s - jnp.max(s, axis=-1, keepdims=True)).astype(BF16)
            vx = jnp.concatenate([vp, jnp.ones((WT, 128), BF16)], 1)
            o = jnp.dot(e, vx, preferred_element_type=F32)
            num = jnp.where(first, o[:size, :128], o[size:, :128])
            den = jnp.where(first, o[:size, 128:], o[size:, 128:])
            parts.append((num / den).astype(BF16))
        att = jnp.concatenate(parts, 1)
        proj = jnp.dot(att, wout[...], preferred_element_type=F32) + b_out[...]
        return proj.astype(BF16).astype(F32)

    def token(l, i):
        return WLON * (WLAT * l + i)

    def compute(r, slot):
        x = jnp.concatenate([win_in[slot, t].astype(BF16) for t in range(LT)], 1)
        proj = attend(biasf.at[r], x)
        for t in range(LT):
            win_out[slot, t] = proj[:, 128 * t : 128 * (t + 1)]

    def take(slot, i0, i1, row0, col):
        for l in range(LEV):
            for i in range(i0, i1):
                j = token(l, i)
                win_in[slot, :, j : j + WLON, :] = fx[:, l, row0 + i - i0, col : col + WLON, :]

    def keep(slot, i1, row0, col, own):
        for l in range(LEV):
            for i in range(i1):
                j = token(l, i)
                pf[:, l, row0 + i, col : col + own, :] = win_out[slot, :, j : j + own, :]

    def pack(slot, i0, i1, off, width, dst, n):
        for l in range(LEV):
            for i in range(i0, i1):
                j = token(l, i) + off
                dst[:, n : n + width, :] = win_out[slot, :, j : j + width, :]
                n += width

    def window_m(b):
        slot = b % 2
        col = SLON + WLON * b
        take(slot, 0, WLAT, 3, col)
        compute(0, slot)
        keep(slot, WLAT, 3, col, WLON if b < 3 else SLON)
        if b == 3:
            pack(slot, 0, WLAT, SLON, SLON, cmp_f.at[0], 0)
            narrow(cmp_f.at[0], s80.at[1], 0, 80)
            wm.start()

    def window_s(b):
        slot = b % 2
        col = SLON + WLON * b
        take(slot, 0, SLAT, 9, col)
        for l in range(LEV):
            j = token(l, SLAT)
            if b < 3:
                n = X_WINDOW + 72 * b + 36 * l
                win_in[slot, :, j : j + 36, :] = stage[:, n : n + 36, :]
            else:
                for i in range(SLAT):
                    n = SLON * (SLAT * l + i)
                    jj = j + WLON * i
                    win_in[slot, :, jj : jj + SLON, :] = stage[
                        :, X_CORNER_E + n : X_CORNER_E + n + SLON, :
                    ]
                    win_in[slot, :, jj + SLON : jj + WLON, :] = cmp_f[1, :, n : n + SLON, :]
        compute(1, slot)

        @pl.when(not_tail)
        def _():
            if b == 3:
                pack(slot, SLAT, WLAT, 0, SLON, stage_r, R_CORNER)
            else:
                for l in range(LEV):
                    n, j = 72 * b + 36 * l, token(l, SLAT)
                    stage_r[:, n : n + 36, :] = win_out[slot, :, j : j + 36, :]
            narrow(stage_r, rs, *R_CUTS[b])
            if b == 3:
                r_copy(b).start()
                pack(slot, SLAT, WLAT, SLON, SLON, cmp_f.at[0], 0)
                narrow(cmp_f.at[0], s48.at[2], 0, 48)
                diag.start()
            elif b == 2:
                r_copy(b).start()
            else:
                pl.when(early_send)(r_copy(b).start)

        if b == 3:
            pack(slot, 0, SLAT, SLON, SLON, cmp_f.at[1], 0)
            narrow(cmp_f.at[1], s48.at[1], 0, 48)
            ws.start()
        keep(slot, SLAT, 9, col, WLON if b < 3 else SLON)

    def window_n(b):
        slot = b % 2
        col = SLON + WLON * b
        for l in range(LEV):
            for i in range(SLAT):
                j = token(l, SLAT + i)
                piece = fx[:, l, i, col : col + WLON, :]
                win_in[slot, :, j : j + WLON, :] = piece
                n = 36 * l + WLON * i
                win_q[slot, :, n : n + WLON, :] = piece
            j = token(l, 0)
            if b < 3:
                n = X_WINDOW + 72 * b + 36 * l
                win_in[slot, :, j : j + 36, :] = stage_n[:, n : n + 36, :]
            else:
                for i in range(SLAT):
                    n = SLON * (SLAT * l + i)
                    jj = j + WLON * i
                    win_in[slot, :, jj : jj + SLON, :] = stage_n[
                        :, X_CORNER_E + n : X_CORNER_E + n + SLON, :
                    ]
                    win_in[slot, :, jj + SLON : jj + WLON, :] = cmp_f[1, :, n : n + SLON, :]
        win_q[slot, :, HALF:HALF_ROWS, :] = jnp.zeros((LT, HALF_ROWS - HALF, 128), F32)
        x = jnp.concatenate([win_in[slot, t].astype(BF16) for t in range(LT)], 1)
        queries = jnp.concatenate([win_q[slot, t].astype(BF16) for t in range(LT)], 1)
        proj = attend(bias_n, x, queries)
        for t in range(LT):
            win_out[slot, t, 0:HALF_ROWS] = proj[:, 128 * t : 128 * (t + 1)]
        own = WLON if b < 3 else SLON
        for l in range(LEV):
            for i in range(SLAT):
                j = 36 * l + WLON * i
                pf[:, l, i, col : col + own, :] = win_out[slot, :, j : j + own, :]
                if b == 3:
                    n = SLON * (SLAT * l + i)
                    cmp_f[0, :, n : n + SLON, :] = win_out[slot, :, j + SLON : j + WLON, :]
        if b == 3:
            narrow(cmp_f.at[0], s48.at[4], 0, 48)
            wn.start()

    loads[C_WQKV].wait()
    loads[C_WOUT].wait()
    loads[C_B].wait()
    def x_take(k):
        x_direct(k).wait_recv()
        x_other(k).wait_recv()
        widen(xr, stage, *X_CUTS[k][::2])

    def last_of_first_band():
        em.wait_recv()
        unpack_east(r80.at[0], 0, 3, 9, 80)
        window_m(3)

    def step_of_sends(k):
        pl.when(early_send)(lambda: x_send(k))

    window_m(0)
    step_of_sends(2)
    window_m(1)
    pl.when(tail)(lambda: t_send(1))
    step_of_sends(3)
    x_relay(0)
    window_m(2)
    pl.when(tail)(lambda: t_send(2))
    x_relay(1)
    pl.when(early_send)(last_of_first_band)
    pl.when(tail)(lambda: t_send(3))
    x_relay(2)
    x_relay(3)

    t_relay(0, forward_first)

    x_take(0)
    pl.when(early_send)(corner.start)
    x_take(1)
    window_s(0)
    t_relay(1, forward_first)
    x_take(2)
    window_s(1)
    t_relay(2, forward_first)
    @pl.when(late_send)
    def _():
        greet_and_send()
        corner.start()
        r_copy(0).start()
        r_copy(1).start()
        x_send(2)
        x_send(3)

    x_take(3)
    window_s(2)
    t_relay(3, forward_first)
    pl.when(late_send)(last_of_first_band)
    es.wait_recv()
    unpack_east(r48.at[0], 0, 9, 12, 48)
    corner.wait_recv()
    widen(cor, cmp_f.at[1], 0, 48)
    window_s(3)

    loads[C_G].wait()
    loads[C_H].wait()

    def finish(row0, row1):
        for l in range(LEV):
            for row in range(row0, row1):
                v = jnp.concatenate([pf[t, l, row] for t in range(LT)], 1)
                mean = jnp.mean(v, axis=-1, keepdims=True)
                d = v - mean
                var = jnp.mean(d * d, axis=-1, keepdims=True)
                normed = d * lax.rsqrt(var + F32(1e-5)) * gain[...] + shift[...]
                out_v[l, row] = (lat_v[l, row].astype(F32) + normed).astype(BF16)

    def place_rows(src, n, width, row0, count, col):
        for l in range(LEV):
            for i in range(count):
                pf[:, l, row0 + i, col : col + width, :] = src[:, n : n + width, :]
                n += width

    def finish_own():
        wm.wait_recv()
        widen(r80.at[1], cmp_f.at[0], 0, 80)
        place_rows(cmp_f.at[0], 0, SLON, 3, WLAT, 0)
        finish(3, 9)
        ws.wait_recv()
        widen(r48.at[1], cmp_f.at[0], 0, 48)
        place_rows(cmp_f.at[0], 0, SLON, 9, SLAT, 0)
        finish(9, 12)

    t_relay(0, forward_last)
    pl.when(not_head)(finish_own)

    @pl.when(not_head)
    def _():
        diag.wait_recv()
        widen(r48.at[2], cmp_f.at[1], 0, 48)
        place_rows(cmp_f.at[1], 0, SLON, 0, SLAT, 0)
        groups = [(36 * l + WLON * i + 72 * b, WLON, l, i, SLON + WLON * b)
                  for b in range(3) for l in range(LEV) for i in range(SLAT)]
        groups += [(R_CORNER + SLON * (SLAT * l + i), SLON, l, i, 42) for l in range(LEV) for i in range(SLAT)]
        for k in range(4):
            r_copy(k).wait_recv()
            a, b = R_CUTS[k]
            widen(rr, stage, a, b)
            for n, width, l, i, col in groups:
                if a < n + width <= b:
                    pf[:, l, i, col : col + width, :] = stage[:, n : n + width, :]

    @pl.when(head)
    def _():
        def t_take(k):
            t_direct(k).wait_recv()
            t_forward(k).wait_recv()
            if k == 0:
                corner_n.start()
            widen(rr, stage_n, *X_CUTS[k][::2])

        b_direct.wait_recv()
        b_pair.start()
        t_take(0)
        t_relay(1, forward_last)
        b_pair.wait_recv()
        for src, side in ((br, core), (bp, 1 - core)):
            bstage[...] = src[...].astype(F32)
            for g in range(4):
                bt[4 * side + g, 0:HALF, :] = bstage[HALF * g : HALF * (g + 1), :]
            for c in range(2):
                @pl.when(side == c)
                def _():
                    bt[HEADS, 36 * c : 36 * (c + 1), :] = bstage[4 * HALF : 4 * HALF + 36, :]
        key = lax.broadcasted_iota(jnp.int32, (HALF, WT), 1)
        south_key = jnp.logical_or(jnp.logical_and(key >= 36, key < 72), key >= 108)
        at_pole = jnp.logical_and(jnp.logical_not(south_key), ilat == 0)
        pole = jnp.where(at_pole, F32(-1e30), F32(0.0))
        for h in range(HEADS):
            n = HALF_ROWS * (h % 2)
            rest = bt[HEADS, 0:HALF, :][:, 16 * h : 16 * (h + 1)]
            bias_n[h // 2, n : n + HALF, :] = jnp.concatenate([bt[h, 0:HALF, :], rest], 1) + pole
            bias_n[h // 2, n + HALF : n + HALF_ROWS, :] = jnp.zeros((HALF_ROWS - HALF, WT), F32)
        en.wait_recv()
        unpack_east(r48.at[3], 0, 0, 3, 48)
        corner_n.wait_recv()
        widen(corn, cmp_f.at[1], 0, 48)
        t_relay(2, forward_last)
        t_relay(3, forward_last)
        window_n(3)
        finish_own()
        for b in range(3):
            t_take(b + 1)
            window_n(b)
        wn.wait_recv()
        widen(r48.at[4], cmp_f.at[1], 0, 48)
        place_rows(cmp_f.at[1], 0, SLON, 0, SLAT, 0)

    finish(0, 3)

    for copy in (em, es, corner, wm, ws):
        copy.wait_send()
    for k in range(4):
        x_direct(k).wait_send()
        x_other(k).wait_send()

    @pl.when(not_tail)
    def _():
        diag.wait_send()
        for k in range(4):
            r_copy(k).wait_send()

    @pl.when(tail)
    def _():
        b_direct.wait_send()
        for k in range(4):
            x_forward(k).wait_send()
            t_direct(k).wait_send()
            t_around(k).wait_send()

    @pl.when(head)
    def _():
        for copy in (en, wn, corner_n, b_pair):
            copy.wait_send()
        for k in range(4):
            t_forward(k).wait_send()


def local_step(nlat, nlon, latent, w_qkv, w_out, b_out, norm_gain, norm_shift, earth_bias):
    hbm = pl.BlockSpec(memory_space=pl.ANY)
    tile = latent.shape
    return pl.pallas_call(
        functools.partial(kernel, nlat, nlon),
        out_shape=pltpu.VMEM(tile, BF16),
        in_specs=[hbm] * 7,
        out_specs=pl.BlockSpec(memory_space=pltpu.VMEM),
        scratch_shapes=[
            pltpu.VMEM(tile, BF16),
            pltpu.VMEM((D, 3 * D), BF16),
            pltpu.VMEM((D, D), BF16),
            pltpu.VMEM((1, D), F32),
            pltpu.VMEM((1, D), F32),
            pltpu.VMEM((1, D), F32),
            pltpu.VMEM((2, HEADS, WT, WT), BF16),
            pltpu.VMEM((2, HEADS // 2, 2 * WT, WT), F32),
            pltpu.VMEM((HEADS // 2, 2 * HALF_ROWS, WT), F32),
            pltpu.VMEM((LT, LEV, 12, 64, 128), F32),
            pltpu.VMEM((LT, LEV, 12, 48, 128), F32),
            pltpu.VMEM((2, LT, WT, 128), F32),
            pltpu.VMEM((2, LT, HALF_ROWS, 128), F32),
            pltpu.VMEM((2, LT, WT, 128), F32),
            pltpu.VMEM((LT, 288, 128), F32),
            pltpu.VMEM((LT, 288, 128), F32),
            pltpu.VMEM((LT, 256, 128), F32),
            pltpu.VMEM((288, D), BF16),
            pltpu.VMEM((288, D), BF16),
            pltpu.VMEM((288, D), BF16),
            pltpu.VMEM((288, D), BF16),
            pltpu.VMEM((288, D), BF16),
            pltpu.VMEM((288, D), BF16),
            pltpu.VMEM((HEADS + 1, WT, 128), F32),
            pltpu.VMEM((B_ROWS, 128), F32),
            pltpu.VMEM((B_ROWS, 128), BF16),
            pltpu.VMEM((B_ROWS, 128), BF16),
            pltpu.VMEM((B_ROWS, 128), BF16),
            pltpu.VMEM((2, LT, 80, 128), F32),
            pltpu.VMEM((2, 80, D), BF16),
            pltpu.VMEM((5, 48, D), BF16),
            pltpu.VMEM((2, 80, D), BF16),
            pltpu.VMEM((5, 48, D), BF16),
            pltpu.VMEM((48, D), BF16),
            pltpu.VMEM((48, D), BF16),
            pltpu.SemaphoreType.DMA((9,)),
            pltpu.SemaphoreType.DMA((COPIES,)),
            pltpu.SemaphoreType.DMA((COPIES,)),
        ],
        compiler_params=pltpu.CompilerParams(
            collective_id=0, has_side_effects=True, vmem_limit_bytes=60 * 1024 * 1024
        ),
        name="swin_window_attention",
    )(
        latent, w_qkv, w_out, b_out.reshape(1, D), norm_gain.reshape(1, D),
        norm_shift.reshape(1, D), earth_bias,
    )


def solution(mesh):
    placed = (P(None, "lat", "lon", None), P(), P(), P(), P(), P(), P("lat", None, None, None))
    step = functools.partial(local_step, mesh.shape["lat"], mesh.shape["lon"])
    return jax.shard_map(
        step, mesh=mesh, in_specs=placed, out_specs=P(None, "lat", "lon", None), check_vma=False
    )
```
